512 devices in a mesh: gx: 32 (over z, y_hi, core), gy: 16 (over y_lo, x).
Axes of the slice: x: 4, y: 8 (y_hi: 2, y_lo: 4; y = y_hi * 4 + y_lo), z: 8, core: 2. Of those that a mesh axis runs over, the one named last changes fastest.
Arguments:
- hidden_in: bfloat16 [32, 14336], P('gy', 'gx'), may hold values from -6 to 6
- ln_gain: float32 [14336], P('gx'), may hold values from 0.1 to 1.9
- w_qkv: bfloat16 [14336, 3, 8192], P('gx', None, 'gy'), may hold values from -0.58463397 to 0.58463397
- slopes: float32 [64], P('gy'), may hold values from 0.00024414062 to 0.12
- k_cache: bfloat16 [32, 64, 1024, 128], P('gx', 'gy'), may hold values from -6 to 6
- v_cache: bfloat16 [32, 64, 1024, 128], P('gx', 'gy'), may hold values from -6 to 6
- lengths: int32 [32], P('gx'), may hold values from 512 to 1024, as said below
- w_out: bfloat16 [8192, 14336], P('gy', 'gx'), may hold values from -0.25 to 0.25
Outputs:
- attn_out: bfloat16 [32, 14336], P('gy', 'gx')
The draws below stay inside these ranges and needn't reach their ends.
Inputs may be any that keep to these rules, and one draw needn't show every extreme that they name: `lengths`: every row has at least 512 live slots; some row has all 1024.
All inputs are finite; a program needn't handle non-finite values.
Results may differ from the reference program's by a relative error of at most 0.009.
The reference program's roundings to bfloat16 on the way (of `normed`, `qkv`, `weights` and `heads_out`) count: a program that leaves them out, or rounds other values in their place, can miss the bound.
Values may be sent and summed in bfloat16 or wider, within the bound.
A program may use at most 64 MiB of HBM per device.

```python
import jax
import jax.numpy as jnp
from jax import lax

D = 14336
HEAD_DIM = 128
HEADS_DEV = 4
ROWS = 32
CACHE = 1024
HEADS = 64


def draw_w_qkv(key, part):
    key = jax.random.fold_in(key, 11)
    shape = (D, 3, HEADS * HEAD_DIM)
    base = jnp.clip(jax.random.normal(key, shape, jnp.float32), -6.0, 6.0)
    return (base / jnp.sqrt(jnp.float32(D))).astype(jnp.bfloat16)


def draw_slopes(key, part):
    key = jax.random.fold_in(key, 23)
    low = jnp.log(0.25 / CACHE)
    high = jnp.log(0.12)
    unit = jax.random.uniform(key, (HEADS,), jnp.float32)
    return jnp.exp(low + (high - low) * unit).astype(jnp.float32)


def draw_lengths(key, part):
    key = jax.random.fold_in(key, 37)
    values = jax.random.randint(key, (ROWS,), CACHE // 2, CACHE + 1)
    where_full = jax.random.randint(jax.random.fold_in(key, 2), (), 0, ROWS)
    return values.at[where_full].set(CACHE).astype(jnp.int32)


def block_scale(rng, extent, pieces, least, high):
    level = 1.0
    for dim, shards_of in pieces:
        heights = jax.random.uniform(jax.random.fold_in(jax.random.fold_in(rng, 6), dim), (shards_of,), jnp.float32, least / len(pieces), high / len(pieces))
        level = level * jnp.repeat(jnp.exp(heights), extent[dim] // shards_of).reshape((-1,) + (1,) * (len(extent) - 1 - dim))
    return level


def noise(stream_key, extent, width, most, pieces=(), held_as=jnp.bfloat16):
    array = jax.random.normal(stream_key, extent, jnp.float32) * width
    if len(pieces) > 0:
        array = block_scale(stream_key, extent, pieces, -0.22, 0.18) * array
    return jnp.clip(array, min=-most, max=most).astype(held_as)


def setup_inputs(seed: int = 0) -> dict:
    arg_keys = jax.random.split(jax.random.key(seed), 9)
    return {
        "hidden_in": noise(arg_keys[0], (ROWS, D), 1.0, 6.0, ((0, 16), (1, 32))),
        "ln_gain": jnp.clip(1.0 + 0.18 * jax.random.normal(arg_keys[1], (D,), jnp.float32), 0.1, 1.9),
        "w_qkv": draw_w_qkv(jax.random.fold_in(arg_keys[8], 71), 0),
        "slopes": draw_slopes(jax.random.fold_in(arg_keys[8], 71), 0),
        "k_cache": noise(arg_keys[4], (ROWS, HEADS, CACHE, HEAD_DIM), 1.0, 6.0, ((0, 32), (1, 16))),
        "v_cache": noise(arg_keys[5], (ROWS, HEADS, CACHE, HEAD_DIM), 1.0, 6.0, ((0, 32), (1, 16))),
        "lengths": draw_lengths(jax.random.fold_in(arg_keys[8], 71), 0),
        "w_out": noise(arg_keys[7], (HEADS * HEAD_DIM, D), (HEADS_DEV * HEAD_DIM) ** -0.5, 0.25, ((0, 16), (1, 32))),
    }


def reference(hidden_in, ln_gain, w_qkv, slopes, k_cache, v_cache, lengths, w_out):
    xf = hidden_in.astype(jnp.float32)
    mean = lax.optimization_barrier(jnp.mean(xf, axis=1, keepdims=True))
    var = lax.optimization_barrier(jnp.mean((xf - mean) * (xf - mean), axis=1, keepdims=True))
    normed = ((xf - mean) * lax.rsqrt(var + 1e-05) * ln_gain[None, :]).astype(jnp.bfloat16)
    flat_w = w_qkv.reshape(D, 3 * HEADS * HEAD_DIM)
    qkv = jnp.dot(normed, flat_w, preferred_element_type=jnp.float32).astype(jnp.bfloat16)
    qkv = qkv.reshape(ROWS, 3, HEADS, HEAD_DIM)
    query = qkv[:, 0]
    key_new = qkv[:, 1]
    value_new = qkv[:, 2]
    scale = 1.0 / jnp.sqrt(jnp.float32(HEAD_DIM))

    def per_row(args):
        q_row, k_row, v_row, keys, values, length = args
        positions = jnp.arange(CACHE, dtype=jnp.int32)
        valid = positions < length
        dist = (length - positions).astype(jnp.float32)
        scores = jnp.einsum('hd,hpd->hp', q_row.astype(jnp.float32), keys.astype(jnp.float32)) * scale
        scores = scores - slopes[:, None] * dist[None, :]
        scores = jnp.where(valid[None, :], scores, jnp.float32(-1e+30))
        own = lax.optimization_barrier(jnp.sum(q_row.astype(jnp.float32) * k_row.astype(jnp.float32), axis=1)) * scale
        top = jnp.maximum(lax.optimization_barrier(jnp.max(scores, axis=1)), own)
        weights = jnp.where(valid[None, :], jnp.exp(scores - top[:, None]), jnp.float32(0.0)).astype(jnp.bfloat16)
        own_weight = jnp.exp(own - top).astype(jnp.bfloat16).astype(jnp.float32)
        total = lax.optimization_barrier(jnp.sum(weights.astype(jnp.float32), axis=1)) + own_weight
        acc = jnp.einsum('hp,hpd->hd', weights.astype(jnp.float32), values.astype(jnp.float32))
        acc = acc + own_weight[:, None] * v_row.astype(jnp.float32)
        return (acc / total[:, None]).astype(jnp.bfloat16)
    heads_out = lax.map(per_row, (query, key_new, value_new, k_cache, v_cache, lengths.astype(jnp.int32)))
    heads_out = heads_out.reshape(ROWS, HEADS * HEAD_DIM)
    return jnp.dot(heads_out, w_out, preferred_element_type=jnp.float32).astype(jnp.bfloat16)
```

```python
import jax
import jax.numpy as jnp
from jax import lax
from jax.experimental import pallas as pl
from jax.experimental.pallas import tpu as pltpu
from jax.sharding import PartitionSpec as P

D = 14336
GX, GY = 32, 16
ROWS, COLS = 32, 448
HEADS, HD, SPAN = 4, 128, 1024
F32, BF16 = jnp.float32, jnp.bfloat16

CORE, YHI, Z = 16, 32, 64
M_ZC = tuple(16 * c + 64 * z for z in range(8) for c in range(2) if c + z)
M_XY = tuple(32 * y + g for y in range(2) for g in range(16) if y + g)
M_GY = tuple(range(1, 16))
M_ZY = tuple(32 * i for i in range(1, 16))
M_GX = tuple(16 * i for i in range(1, 32))


def kernel(
    x_hbm, gain_hbm, w_hbm, k_hbm, v_hbm, wo_hbm, slopes, lengths, out_ref,
    x_v, gain_v, w_v, k_v, v_v, wo_v,
    xsend, xrecv, a_send, a_recv, b_recv, xs, st,
    part, sib, zy_send, zy_recv, h_recv, h_flat, o_send, o_recv,
    local_sem, send_sem, recv_sem,
):
    gx, gy = lax.axis_index("gx"), lax.axis_index("gy")
    me = gx * GY + gy
    core = gx & 1

    def load(n, src, dst):
        copy = pltpu.make_async_copy(src, dst, local_sem.at[n])
        copy.start()
        return copy

    def send(n, src, dst, mask):
        pltpu.make_async_remote_copy(
            src_ref=src, dst_ref=dst, send_sem=send_sem.at[n], recv_sem=recv_sem.at[n],
            device_id=me ^ mask, device_id_type=pl.DeviceIdType.LOGICAL,
        ).start()

    def arrived(n, ref):
        pltpu.make_async_copy(ref, ref, recv_sem.at[n]).wait()

    def sent(n, ref):
        pltpu.make_async_copy(ref, ref, send_sem.at[n]).wait()

    get_x = load(0, x_hbm, x_v)
    barrier = pltpu.get_barrier_semaphore()
    for mask in M_ZC + M_XY:
        pl.semaphore_signal(
            barrier, inc=1, device_id=me ^ mask, device_id_type=pl.DeviceIdType.LOGICAL
        )
    get_gain = load(1, gain_hbm, gain_v)
    get_w = [load(2 + c, w_hbm.at[c], w_v.at[c]) for c in range(3)]
    get_k = [load(5 + h, k_hbm.at[h], k_v.at[:, pl.ds(h * HD, HD)]) for h in range(HEADS)]
    get_v = [load(9 + h, v_hbm.at[h], v_v.at[:, pl.ds(h * HD, HD)]) for h in range(HEADS)]
    get_wo = load(13, wo_hbm, wo_v)

    get_x.wait()
    xf = x_v[...].astype(F32)
    low2 = lax.broadcasted_iota(jnp.int32, (2, 128), 1) < 64
    stats = jnp.where(
        low2, jnp.sum(xf, axis=1, keepdims=True), jnp.sum(xf * xf, axis=1, keepdims=True)
    )
    a_send[0] = stats
    xsend[...] = xf
    xrecv[gy] = xf
    pl.semaphore_wait(barrier, len(M_ZC) + len(M_XY))

    for n, mask in enumerate(M_ZC):
        send(0, a_send.at[0], a_recv.at[n], mask)
    for mask in M_GY:
        send(1, xsend, xrecv.at[gy], mask)
    arrived(0, a_recv)
    stats = stats + jnp.sum(a_recv[...], axis=0)

    slot = ((gx >> 1) & 1) * GY + gy
    a_send[1] = stats
    b_recv[slot] = stats
    for mask in M_XY:
        send(2, a_send.at[1], b_recv.at[slot], mask)
    arrived(1, xrecv.at[pl.ds(0, GY - 1)])
    for j in range(GY):
        for t in range(2):
            xs[t * GY + j : t * GY + j + 1, :] = xrecv[j, t : t + 1, :]
    get_gain.wait()
    for c in get_w:
        c.wait()
    arrived(2, b_recv.at[pl.ds(0, 2 * GY - 1)])
    for j in range(GY):
        both = b_recv[j] + b_recv[GY + j]
        for t in range(2):
            st[t * GY + j : t * GY + j + 1, :] = both[t : t + 1, :]
    tot = st[...]
    other = pltpu.roll(tot, 64, 1)
    low = lax.broadcasted_iota(jnp.int32, (ROWS, 128), 1) < 64
    mean = jnp.where(low, tot, other) * (1.0 / D)
    var = jnp.where(low, other, tot) * (1.0 / D) - mean * mean
    rstd = lax.rsqrt(var + 1e-05)
    pieces = []
    for c in range(0, COLS, 128):
        wide = min(128, COLS - c)
        piece = (xs[:, c : c + wide] - mean[:, :wide]) * rstd[:, :wide]
        pieces.append((piece * gain_v[:, c : c + wide]).astype(BF16))
    normed = jnp.concatenate(pieces, axis=1)

    for c in range(3):
        res = jnp.dot(normed, w_v[c], preferred_element_type=F32)
        part[c, 0] = res[:GY]
        part[c, 1] = res[GY:]
        send(3 + c, part.at[c, 1 - core], sib.at[c], CORE)
    for c in range(3):
        arrived(3 + c, sib.at[c])
        mine = part[c, core] + sib[c]
        for h in range(HEADS):
            zy_send[:, c * HEADS + h, :] = mine[:, h * HD : (h + 1) * HD]
    own_slot = gx >> 1
    for n, mask in enumerate(M_ZY):
        send(6, zy_send.at[own_slot ^ (mask >> 5)], zy_recv.at[n], mask)

    length = lengths[0]
    row8 = lax.broadcasted_iota(jnp.int32, (8, 1), 0)
    slope = jnp.zeros((8, 1), F32)
    for h in range(HEADS):
        slope = jnp.where(row8 == h, slopes[h], slope)
    position = lax.broadcasted_iota(jnp.int32, (8, SPAN), 1)
    valid = position < length
    bias = slope * (length - position).astype(F32)
    for c in get_k + get_v:
        c.wait()
    get_wo.wait()
    arrived(6, zy_recv)
    qkv = (zy_send[own_slot] + jnp.sum(zy_recv[...], axis=0)).astype(BF16).astype(F32)
    q, k_new, v_new = qkv[0:4], qkv[4:8], qkv[8:12]
    scale = 1.0 / jnp.sqrt(jnp.float32(HD))
    row4 = lax.broadcasted_iota(jnp.int32, (HEADS, HD), 0)
    q_blocks = jnp.concatenate([jnp.where(row4 == h, q, 0.0) for h in range(HEADS)], axis=1)
    q_blocks = jnp.concatenate([q_blocks, jnp.zeros_like(q_blocks)], axis=0).astype(BF16)
    nt = (((1,), (1,)), ((), ()))
    scores = lax.dot_general(q_blocks, k_v[...], nt, preferred_element_type=F32) * scale - bias
    scores = jnp.where(valid, scores, -1e30)
    own = jnp.sum(q * k_new, axis=1, keepdims=True) * scale
    own = jnp.concatenate([own, jnp.zeros_like(own)], axis=0)
    top = jnp.maximum(jnp.max(scores, axis=1, keepdims=True), own)
    weights = jnp.where(valid, jnp.exp(scores - top), 0.0).astype(BF16)
    own_weight = jnp.exp(own - top).astype(BF16).astype(F32)
    total = jnp.sum(weights.astype(F32), axis=1, keepdims=True) + own_weight
    mixed = jnp.dot(weights, v_v[...], preferred_element_type=F32)
    acc = own_weight[:HEADS] * v_new
    for h in range(HEADS):
        acc = acc + jnp.where(row4 == h, mixed[:HEADS, h * HD : (h + 1) * HD], 0.0)
    heads = (acc / total[:HEADS]).astype(BF16).astype(F32)

    h_recv[gx] = heads
    for mask in M_GX:
        send(7, h_recv.at[gx], h_recv.at[gx], mask)
    arrived(7, h_recv.at[pl.ds(0, GX - 1)])
    for r in range(GX):
        h_flat[r * HEADS : (r + 1) * HEADS, :] = h_recv[r]
    lhs = jnp.concatenate(
        [h_flat[pl.ds(h, GX, stride=HEADS), :].astype(BF16) for h in range(HEADS)], axis=1
    )
    res = lax.dot_general(lhs, wo_v[...], nt, preferred_element_type=F32)

    for j in range(GY):
        o_send[j] = res[2 * j : 2 * j + 2]
    for n, mask in enumerate(M_GY):
        send(8, o_send.at[gy ^ mask], o_recv.at[n], mask)
    arrived(8, o_recv)
    out_ref[...] = (o_send[gy] + jnp.sum(o_recv[...], axis=0)).astype(BF16)

    sent(0, a_recv)
    sent(1, xrecv.at[pl.ds(0, GY - 1)])
    sent(2, b_recv.at[pl.ds(0, 2 * GY - 1)])
    for c in range(3):
        sent(3 + c, sib.at[c])
    sent(6, zy_recv)
    sent(7, h_recv.at[pl.ds(0, GX - 1)])
    sent(8, o_recv)


def local(hidden_in, ln_gain, w_qkv, slopes, k_cache, v_cache, lengths, w_out):
    hbm = pl.BlockSpec(memory_space=pltpu.HBM)
    smem = pl.BlockSpec(memory_space=pltpu.SMEM)
    return pl.pallas_call(
        kernel,
        out_shape=jax.ShapeDtypeStruct((2, COLS), BF16),
        in_specs=[hbm] * 6 + [smem] * 2,
        out_specs=pl.BlockSpec(memory_space=pltpu.VMEM),
        scratch_shapes=[
            pltpu.VMEM((2, COLS), BF16),
            pltpu.VMEM((1, COLS), F32),
            pltpu.VMEM((3, COLS, HEADS * HD), BF16),
            pltpu.VMEM((SPAN, HEADS * HD), BF16),
            pltpu.VMEM((SPAN, HEADS * HD), BF16),
            pltpu.VMEM((COLS, HEADS * HD), BF16),
            pltpu.VMEM((2, COLS), F32),
            pltpu.VMEM((GY, 2, COLS), F32),
            pltpu.VMEM((2, 2, 128), F32),
            pltpu.VMEM((len(M_ZC), 2, 128), F32),
            pltpu.VMEM((2 * GY, 2, 128), F32),
            pltpu.VMEM((ROWS, COLS), F32),
            pltpu.VMEM((ROWS, 128), F32),
            pltpu.VMEM((3, 2, GY, HEADS * HD), F32),
            pltpu.VMEM((3, GY, HEADS * HD), F32),
            pltpu.VMEM((GY, 3 * HEADS, HD), F32),
            pltpu.VMEM((len(M_ZY), 3 * HEADS, HD), F32),
            pltpu.VMEM((GX, HEADS, HD), F32),
            pltpu.VMEM((GX * HEADS, HD), F32),
            pltpu.VMEM((GY, 2, COLS), F32),
            pltpu.VMEM((len(M_GY), 2, COLS), F32),
            pltpu.SemaphoreType.DMA((14,)),
            pltpu.SemaphoreType.DMA((9,)),
            pltpu.SemaphoreType.DMA((9,)),
        ],
        compiler_params=pltpu.CompilerParams(
            collective_id=0, has_side_effects=True, vmem_limit_bytes=32 * 1024 * 1024
        ),
        name="decode_attention",
    )(
        hidden_in,
        ln_gain.reshape(1, COLS),
        jnp.transpose(w_qkv, (1, 0, 2)),
        k_cache.reshape(HEADS, SPAN, HD),
        v_cache.reshape(HEADS, SPAN, HD),
        w_out.T,
        slopes,
        lengths,
    )


def solution(mesh):
    in_specs = (
        P("gy", "gx"),
        P("gx"),
        P("gx", None, "gy"),
        P("gy"),
        P("gx", "gy", None, None),
        P("gx", "gy", None, None),
        P("gx"),
        P("gy", "gx"),
    )
    out_specs = P("gy", "gx")
    return jax.shard_map(local, mesh=mesh, in_specs=in_specs, out_specs=out_specs, check_vma=False)
```

```python
import jax
import jax.numpy as jnp
from jax import lax
from jax.experimental import pallas as pl
from jax.experimental.pallas import tpu as pltpu
from jax.sharding import PartitionSpec as P

D = 14336
GX, GY = 32, 16
ROWS, COLS = 32, 448
HEADS, HD, SPAN = 4, 128, 1024
F32, BF16 = jnp.float32, jnp.bfloat16

CORE, YHI, Z = 16, 32, 64
M_ZC = tuple(16 * c + 64 * z for z in range(8) for c in range(2) if c + z)
M_XY = tuple(32 * y + g for y in range(2) for g in range(16) if y + g)
M_GY = tuple(range(1, 16))
M_ZY = tuple(32 * i for i in range(1, 16))
M_GX = tuple(16 * i for i in range(1, 32))


def kernel(
    x_hbm, gain_hbm, w_hbm, k_hbm, v_hbm, wo_hbm, slopes_hbm, lengths_hbm, out_ref,
    x_v, gain_v, w_v, k_v, v_v, wo_v, slopes_v, lengths_v,
    xsend, xrecv, a_send, a_recv, b_recv, xs, st,
    part, sib, zy_send, zy_recv, h_recv, h_flat, o_send, o_recv,
    local_sem, send_sem, recv_sem,
):
    gx, gy = lax.axis_index("gx"), lax.axis_index("gy")
    me = gx * GY + gy
    core = gx & 1

    def load(n, src, dst):
        copy = pltpu.make_async_copy(src, dst, local_sem.at[n])
        copy.start()
        return copy

    def send(n, src, dst, mask):
        pltpu.make_async_remote_copy(
            src_ref=src, dst_ref=dst, send_sem=send_sem.at[n], recv_sem=recv_sem.at[n],
            device_id=me ^ mask, device_id_type=pl.DeviceIdType.LOGICAL,
        ).start()

    def arrived(n, ref):
        pltpu.make_async_copy(ref, ref, recv_sem.at[n]).wait()

    def sent(n, ref):
        pltpu.make_async_copy(ref, ref, send_sem.at[n]).wait()

    get_x = load(0, x_hbm, x_v)
    barrier = pltpu.get_barrier_semaphore()
    for mask in M_ZC + M_XY:
        pl.semaphore_signal(
            barrier, inc=1, device_id=me ^ mask, device_id_type=pl.DeviceIdType.LOGICAL
        )
    get_gain = load(1, gain_hbm, gain_v)
    get_w = [load(2 + c, w_hbm.at[c], w_v.at[c]) for c in range(3)]
    get_k = [load(5 + h, k_hbm.at[h], k_v.at[:, pl.ds(h * HD, HD)]) for h in range(HEADS)]
    get_v = [load(9 + h, v_hbm.at[h], v_v.at[:, pl.ds(h * HD, HD)]) for h in range(HEADS)]
    get_wo = load(13, wo_hbm, wo_v)
    get_slopes = load(14, slopes_hbm, slopes_v)
    get_lengths = load(15, lengths_hbm, lengths_v)

    get_x.wait()
    xf = x_v[...].astype(F32)
    low2 = lax.broadcasted_iota(jnp.int32, (2, 128), 1) < 64
    stats = jnp.where(
        low2, jnp.sum(xf, axis=1, keepdims=True), jnp.sum(xf * xf, axis=1, keepdims=True)
    )
    a_send[0] = stats
    xsend[...] = xf
    xrecv[gy] = xf
    pl.semaphore_wait(barrier, len(M_ZC) + len(M_XY))

    for n, mask in enumerate(M_ZC):
        send(0, a_send.at[0], a_recv.at[n], mask)
    for mask in M_GY:
        send(1, xsend, xrecv.at[gy], mask)
    arrived(0, a_recv)
    stats = stats + jnp.sum(a_recv[...], axis=0)

    slot = ((gx >> 1) & 1) * GY + gy
    a_send[1] = stats
    b_recv[slot] = stats
    for mask in M_XY:
        send(2, a_send.at[1], b_recv.at[slot], mask)
    arrived(1, xrecv.at[pl.ds(0, GY - 1)])
    for j in range(GY):
        for t in range(2):
            xs[t * GY + j : t * GY + j + 1, :] = xrecv[j, t : t + 1, :]
    get_gain.wait()
    for c in get_w:
        c.wait()
    arrived(2, b_recv.at[pl.ds(0, 2 * GY - 1)])
    for j in range(GY):
        both = b_recv[j] + b_recv[GY + j]
        for t in range(2):
            st[t * GY + j : t * GY + j + 1, :] = both[t : t + 1, :]
    tot = st[...]
    other = pltpu.roll(tot, 64, 1)
    low = lax.broadcasted_iota(jnp.int32, (ROWS, 128), 1) < 64
    mean = jnp.where(low, tot, other) * (1.0 / D)
    var = jnp.where(low, other, tot) * (1.0 / D) - mean * mean
    rstd = lax.rsqrt(var + 1e-05)
    pieces = []
    for c in range(0, COLS, 128):
        wide = min(128, COLS - c)
        piece = (xs[:, c : c + wide] - mean[:, :wide]) * rstd[:, :wide]
        pieces.append((piece * gain_v[:, c : c + wide]).astype(BF16))
    normed = jnp.concatenate(pieces, axis=1)

    for c in range(3):
        res = jnp.dot(normed, w_v[c], preferred_element_type=F32)
        part[c, 0] = res[:GY]
        part[c, 1] = res[GY:]
        send(3 + c, part.at[c, 1 - core], sib.at[c], CORE)
    for c in range(3):
        arrived(3 + c, sib.at[c])
        mine = part[c, core] + sib[c]
        for h in range(HEADS):
            zy_send[:, c * HEADS + h, :] = mine[:, h * HD : (h + 1) * HD]
    own_slot = gx >> 1
    for n, mask in enumerate(M_ZY):
        send(6, zy_send.at[own_slot ^ (mask >> 5)], zy_recv.at[n], mask)

    get_slopes.wait()
    get_lengths.wait()
    length = lengths_v[...]
    diagonal = lax.broadcasted_iota(jnp.int32, (8, HEADS), 0) == lax.broadcasted_iota(
        jnp.int32, (8, HEADS), 1
    )
    slope = jnp.sum(jnp.where(diagonal, slopes_v[...], 0.0), axis=1, keepdims=True)
    position = lax.broadcasted_iota(jnp.int32, (8, SPAN), 1)
    valid = position < length
    bias = slope * (length - position).astype(F32)
    for c in get_k + get_v:
        c.wait()
    get_wo.wait()
    arrived(6, zy_recv)
    qkv = (zy_send[own_slot] + jnp.sum(zy_recv[...], axis=0)).astype(BF16).astype(F32)
    q, k_new, v_new = qkv[0:4], qkv[4:8], qkv[8:12]
    scale = 1.0 / jnp.sqrt(jnp.float32(HD))
    row4 = lax.broadcasted_iota(jnp.int32, (HEADS, HD), 0)
    q_blocks = jnp.concatenate([jnp.where(row4 == h, q, 0.0) for h in range(HEADS)], axis=1)
    q_blocks = jnp.concatenate([q_blocks, jnp.zeros_like(q_blocks)], axis=0).astype(BF16)
    nt = (((1,), (1,)), ((), ()))
    scores = lax.dot_general(q_blocks, k_v[...], nt, preferred_element_type=F32) * scale - bias
    scores = jnp.where(valid, scores, -1e30)
    own = jnp.sum(q * k_new, axis=1, keepdims=True) * scale
    own = jnp.concatenate([own, jnp.zeros_like(own)], axis=0)
    top = jnp.maximum(jnp.max(scores, axis=1, keepdims=True), own)
    weights = jnp.where(valid, jnp.exp(scores - top), 0.0).astype(BF16)
    own_weight = jnp.exp(own - top).astype(BF16).astype(F32)
    total = jnp.sum(weights.astype(F32), axis=1, keepdims=True) + own_weight
    mixed = jnp.dot(weights, v_v[...], preferred_element_type=F32)
    acc = own_weight[:HEADS] * v_new
    for h in range(HEADS):
        acc = acc + jnp.where(row4 == h, mixed[:HEADS, h * HD : (h + 1) * HD], 0.0)
    heads = (acc / total[:HEADS]).astype(BF16).astype(F32)

    h_recv[gx] = heads
    for mask in M_GX:
        send(7, h_recv.at[gx], h_recv.at[gx], mask)
    arrived(7, h_recv.at[pl.ds(0, GX - 1)])
    for r in range(GX):
        h_flat[r * HEADS : (r + 1) * HEADS, :] = h_recv[r]
    lhs = jnp.concatenate(
        [h_flat[pl.ds(h, GX, stride=HEADS), :].astype(BF16) for h in range(HEADS)], axis=1
    )
    res = lax.dot_general(lhs, wo_v[...], nt, preferred_element_type=F32)

    for j in range(GY):
        o_send[j] = res[2 * j : 2 * j + 2]
    for n, mask in enumerate(M_GY):
        send(8, o_send.at[gy ^ mask], o_recv.at[n], mask)
    arrived(8, o_recv)
    out_ref[...] = (o_send[gy] + jnp.sum(o_recv[...], axis=0)).astype(BF16)

    sent(0, a_recv)
    sent(1, xrecv.at[pl.ds(0, GY - 1)])
    sent(2, b_recv.at[pl.ds(0, 2 * GY - 1)])
    for c in range(3):
        sent(3 + c, sib.at[c])
    sent(6, zy_recv)
    sent(7, h_recv.at[pl.ds(0, GX - 1)])
    sent(8, o_recv)


def local(hidden_in, ln_gain, w_qkv, slopes, k_cache, v_cache, lengths, w_out):
    hbm = pl.BlockSpec(memory_space=pltpu.HBM)
    return pl.pallas_call(
        kernel,
        out_shape=jax.ShapeDtypeStruct((2, COLS), BF16),
        in_specs=[hbm] * 8,
        out_specs=pl.BlockSpec(memory_space=pltpu.VMEM),
        scratch_shapes=[
            pltpu.VMEM((2, COLS), BF16),
            pltpu.VMEM((1, COLS), F32),
            pltpu.VMEM((3, COLS, HEADS * HD), BF16),
            pltpu.VMEM((SPAN, HEADS * HD), BF16),
            pltpu.VMEM((SPAN, HEADS * HD), BF16),
            pltpu.VMEM((COLS, HEADS * HD), BF16),
            pltpu.VMEM((1, HEADS), F32),
            pltpu.VMEM((1, 1), jnp.int32),
            pltpu.VMEM((2, COLS), F32),
            pltpu.VMEM((GY, 2, COLS), F32),
            pltpu.VMEM((2, 2, 128), F32),
            pltpu.VMEM((len(M_ZC), 2, 128), F32),
            pltpu.VMEM((2 * GY, 2, 128), F32),
            pltpu.VMEM((ROWS, COLS), F32),
            pltpu.VMEM((ROWS, 128), F32),
            pltpu.VMEM((3, 2, GY, HEADS * HD), F32),
            pltpu.VMEM((3, GY, HEADS * HD), F32),
            pltpu.VMEM((GY, 3 * HEADS, HD), F32),
            pltpu.VMEM((len(M_ZY), 3 * HEADS, HD), F32),
            pltpu.VMEM((GX, HEADS, HD), F32),
            pltpu.VMEM((GX * HEADS, HD), F32),
            pltpu.VMEM((GY, 2, COLS), F32),
            pltpu.VMEM((len(M_GY), 2, COLS), F32),
            pltpu.SemaphoreType.DMA((16,)),
            pltpu.SemaphoreType.DMA((9,)),
            pltpu.SemaphoreType.DMA((9,)),
        ],
        compiler_params=pltpu.CompilerParams(
            collective_id=0, has_side_effects=True, vmem_limit_bytes=62 * 1024 * 1024
        ),
        name="decode_attention",
    )(
        hidden_in,
        ln_gain.reshape(1, COLS),
        jnp.transpose(w_qkv, (1, 0, 2)),
        k_cache.reshape(HEADS, SPAN, HD),
        v_cache.reshape(HEADS, SPAN, HD),
        w_out.T,
        slopes.reshape(1, HEADS),
        lengths.reshape(1, 1),
    )


def solution(mesh):
    in_specs = (
        P("gy", "gx"),
        P("gx"),
        P("gx", None, "gy"),
        P("gy"),
        P("gx", "gy", None, None),
        P("gx", "gy", None, None),
        P("gx"),
        P("gy", "gx"),
    )
    out_specs = P("gy", "gx")
    return jax.shard_map(local, mesh=mesh, in_specs=in_specs, out_specs=out_specs, check_vma=False)
```

```python
import jax
import jax.numpy as jnp
from jax import lax
from jax.experimental import pallas as pl
from jax.experimental.pallas import tpu as pltpu
from jax.sharding import PartitionSpec as P

D = 14336
GX, GY = 32, 16
ROWS, COLS = 32, 448
HEADS, HD, SPAN = 4, 128, 1024
F32, BF16 = jnp.float32, jnp.bfloat16

CORE, YHI, Z = 16, 32, 64
M_ZC = tuple(16 * c + 64 * z for z in range(8) for c in range(2) if c + z)
M_XY = tuple(32 * y + g for y in range(2) for g in range(16) if y + g)
M_GY = tuple(range(1, 16))
M_ZY = tuple(32 * i for i in range(1, 16))
M_GX = tuple(16 * i for i in range(1, 32))


def kernel(
    x_hbm, gain_hbm, w_hbm, k_hbm, v_hbm, wo_hbm, slopes_hbm, lengths_hbm, out_ref,
    x_v, gain_v, w_v, k_v, k_t, v_v, wo_v, wo_t, slopes_v, lengths_v,
    xsend, xrecv, a_send, a_recv, b_recv, xs, st,
    part, sib, zy_send, zy_recv, h_recv, h_flat, o_send, o_recv,
    local_sem, send_sem, recv_sem,
):
    gx, gy = lax.axis_index("gx"), lax.axis_index("gy")
    me = gx * GY + gy
    core = gx & 1

    def load(n, src, dst):
        copy = pltpu.make_async_copy(src, dst, local_sem.at[n])
        copy.start()
        return copy

    def send(n, src, dst, mask):
        pltpu.make_async_remote_copy(
            src_ref=src, dst_ref=dst, send_sem=send_sem.at[n], recv_sem=recv_sem.at[n],
            device_id=me ^ mask, device_id_type=pl.DeviceIdType.LOGICAL,
        ).start()

    def arrived(n, ref):
        pltpu.make_async_copy(ref, ref, recv_sem.at[n]).wait()

    def sent(n, ref):
        pltpu.make_async_copy(ref, ref, send_sem.at[n]).wait()

    get_x = load(0, x_hbm, x_v)
    barrier = pltpu.get_barrier_semaphore()
    for mask in M_ZC + M_XY:
        pl.semaphore_signal(
            barrier, inc=1, device_id=me ^ mask, device_id_type=pl.DeviceIdType.LOGICAL
        )
    get_gain = load(1, gain_hbm, gain_v)
    get_w = [load(2 + c, w_hbm.at[c], w_v.at[c]) for c in range(3)]
    get_k = [load(5 + h, k_hbm.at[h], k_v.at[h]) for h in range(HEADS)]
    get_v = [load(9 + h, v_hbm.at[h], v_v.at[:, pl.ds(h * HD, HD)]) for h in range(HEADS)]
    get_wo = load(13, wo_hbm, wo_v)
    get_slopes = load(14, slopes_hbm, slopes_v)
    get_lengths = load(15, lengths_hbm, lengths_v)

    get_x.wait()
    xf = x_v[...].astype(F32)
    low2 = lax.broadcasted_iota(jnp.int32, (2, 128), 1) < 64
    stats = jnp.where(
        low2, jnp.sum(xf, axis=1, keepdims=True), jnp.sum(xf * xf, axis=1, keepdims=True)
    )
    a_send[0] = stats
    xsend[...] = xf
    xrecv[gy] = xf
    pl.semaphore_wait(barrier, len(M_ZC) + len(M_XY))

    for n, mask in enumerate(M_ZC):
        send(0, a_send.at[0], a_recv.at[n], mask)
    for mask in M_GY:
        send(1, xsend, xrecv.at[gy], mask)
    arrived(0, a_recv)
    stats = stats + jnp.sum(a_recv[...], axis=0)

    slot = ((gx >> 1) & 1) * GY + gy
    a_send[1] = stats
    b_recv[slot] = stats
    for mask in M_XY:
        send(2, a_send.at[1], b_recv.at[slot], mask)
    arrived(1, xrecv.at[pl.ds(0, GY - 1)])
    for j in range(GY):
        for t in range(2):
            xs[t * GY + j : t * GY + j + 1, :] = xrecv[j, t : t + 1, :]
    get_gain.wait()
    for c in get_w:
        c.wait()
    arrived(2, b_recv.at[pl.ds(0, 2 * GY - 1)])
    for j in range(GY):
        both = b_recv[j] + b_recv[GY + j]
        for t in range(2):
            st[t * GY + j : t * GY + j + 1, :] = both[t : t + 1, :]
    tot = st[...]
    other = pltpu.roll(tot, 64, 1)
    low = lax.broadcasted_iota(jnp.int32, (ROWS, 128), 1) < 64
    mean = jnp.where(low, tot, other) * (1.0 / D)
    var = jnp.where(low, other, tot) * (1.0 / D) - mean * mean
    rstd = lax.rsqrt(var + 1e-05)
    pieces = []
    for c in range(0, COLS, 128):
        wide = min(128, COLS - c)
        piece = (xs[:, c : c + wide] - mean[:, :wide]) * rstd[:, :wide]
        pieces.append((piece * gain_v[:, c : c + wide]).astype(BF16))
    normed = jnp.concatenate(pieces, axis=1)

    for c in range(3):
        res = jnp.dot(normed, w_v[c], preferred_element_type=F32)
        part[c, 0] = res[:GY]
        part[c, 1] = res[GY:]
        send(3 + c, part.at[c, 1 - core], sib.at[c], CORE)
    for c in range(3):
        arrived(3 + c, sib.at[c])
        mine = part[c, core] + sib[c]
        for h in range(HEADS):
            zy_send[:, c * HEADS + h, :] = mine[:, h * HD : (h + 1) * HD]
    own_slot = gx >> 1
    for n, mask in enumerate(M_ZY):
        send(6, zy_send.at[own_slot ^ (mask >> 5)], zy_recv.at[n], mask)

    get_slopes.wait()
    get_lengths.wait()
    length = lengths_v[...]
    diagonal = lax.broadcasted_iota(jnp.int32, (8, HEADS), 0) == lax.broadcasted_iota(
        jnp.int32, (8, HEADS), 1
    )
    slope = jnp.sum(jnp.where(diagonal, slopes_v[...], 0.0), axis=1, keepdims=True)
    position = lax.broadcasted_iota(jnp.int32, (8, SPAN), 1)
    valid = position < length
    bias = slope * (length - position).astype(F32)
    for h in range(HEADS):
        get_k[h].wait()
        k_t[h * HD : (h + 1) * HD, :] = k_v[h].T
    get_wo.wait()
    wo_t[...] = wo_v[...].T
    for c in get_v:
        c.wait()
    arrived(6, zy_recv)
    qkv = (zy_send[own_slot] + jnp.sum(zy_recv[...], axis=0)).astype(BF16).astype(F32)
    q, k_new, v_new = qkv[0:4], qkv[4:8], qkv[8:12]
    scale = 1.0 / jnp.sqrt(jnp.float32(HD))
    row4 = lax.broadcasted_iota(jnp.int32, (HEADS, HD), 0)
    q_blocks = jnp.concatenate([jnp.where(row4 == h, q, 0.0) for h in range(HEADS)], axis=1)
    q_blocks = jnp.concatenate([q_blocks, jnp.zeros_like(q_blocks)], axis=0).astype(BF16)
    scores = jnp.dot(q_blocks, k_t[...], preferred_element_type=F32) * scale - bias
    scores = jnp.where(valid, scores, -1e30)
    own = jnp.sum(q * k_new, axis=1, keepdims=True) * scale
    own = jnp.concatenate([own, jnp.zeros_like(own)], axis=0)
    top = jnp.maximum(jnp.max(scores, axis=1, keepdims=True), own)
    weights = jnp.where(valid, jnp.exp(scores - top), 0.0).astype(BF16)
    own_weight = jnp.exp(own - top).astype(BF16).astype(F32)
    total = jnp.sum(weights.astype(F32), axis=1, keepdims=True) + own_weight
    mixed = jnp.dot(weights, v_v[...], preferred_element_type=F32)
    acc = own_weight[:HEADS] * v_new
    for h in range(HEADS):
        acc = acc + jnp.where(row4 == h, mixed[:HEADS, h * HD : (h + 1) * HD], 0.0)
    heads = (acc / total[:HEADS]).astype(BF16)

    h_recv[gx] = heads
    for mask in M_GX:
        send(7, h_recv.at[gx], h_recv.at[gx], mask)
    arrived(7, h_recv.at[pl.ds(0, GX - 1)])
    for r in range(GX):
        h_flat[r * HEADS : (r + 1) * HEADS, :] = h_recv[r].astype(F32)
    lhs = jnp.concatenate(
        [h_flat[pl.ds(h, GX, stride=HEADS), :].astype(BF16) for h in range(HEADS)], axis=1
    )
    res = jnp.dot(lhs, wo_t[...], preferred_element_type=F32)

    for j in range(GY):
        o_send[j] = res[2 * j : 2 * j + 2]
    for n, mask in enumerate(M_GY):
        send(8, o_send.at[gy ^ mask], o_recv.at[n], mask)
    arrived(8, o_recv)
    out_ref[...] = (o_send[gy] + jnp.sum(o_recv[...], axis=0)).astype(BF16)

    sent(0, a_recv)
    sent(1, xrecv.at[pl.ds(0, GY - 1)])
    sent(2, b_recv.at[pl.ds(0, 2 * GY - 1)])
    for c in range(3):
        sent(3 + c, sib.at[c])
    sent(6, zy_recv)
    sent(7, h_recv.at[pl.ds(0, GX - 1)])
    sent(8, o_recv)


def local(hidden_in, ln_gain, w_qkv, slopes, k_cache, v_cache, lengths, w_out):
    hbm = pl.BlockSpec(memory_space=pltpu.HBM)
    return pl.pallas_call(
        kernel,
        out_shape=pltpu.VMEM((2, COLS), BF16),
        in_specs=[hbm] * 8,
        out_specs=pl.BlockSpec(memory_space=pltpu.VMEM),
        scratch_shapes=[
            pltpu.VMEM((2, COLS), BF16),
            pltpu.VMEM((1, COLS), F32),
            pltpu.VMEM((3, COLS, HEADS * HD), BF16),
            pltpu.VMEM((HEADS, SPAN, HD), BF16),
            pltpu.VMEM((HEADS * HD, SPAN), BF16),
            pltpu.VMEM((SPAN, HEADS * HD), BF16),
            pltpu.VMEM((COLS, HEADS * HD), BF16),
            pltpu.VMEM((HEADS * HD, COLS), BF16),
            pltpu.VMEM((1, HEADS), F32),
            pltpu.VMEM((1, 1), jnp.int32),
            pltpu.VMEM((2, COLS), F32),
            pltpu.VMEM((GY, 2, COLS), F32),
            pltpu.VMEM((2, 2, 128), F32),
            pltpu.VMEM((len(M_ZC), 2, 128), F32),
            pltpu.VMEM((2 * GY, 2, 128), F32),
            pltpu.VMEM((ROWS, COLS), F32),
            pltpu.VMEM((ROWS, 128), F32),
            pltpu.VMEM((3, 2, GY, HEADS * HD), F32),
            pltpu.VMEM((3, GY, HEADS * HD), F32),
            pltpu.VMEM((GY, 3 * HEADS, HD), F32),
            pltpu.VMEM((len(M_ZY), 3 * HEADS, HD), F32),
            pltpu.VMEM((GX, HEADS, HD), BF16),
            pltpu.VMEM((GX * HEADS, HD), F32),
            pltpu.VMEM((GY, 2, COLS), F32),
            pltpu.VMEM((len(M_GY), 2, COLS), F32),
            pltpu.SemaphoreType.DMA((16,)),
            pltpu.SemaphoreType.DMA((9,)),
            pltpu.SemaphoreType.DMA((9,)),
        ],
        compiler_params=pltpu.CompilerParams(
            collective_id=0, has_side_effects=True, vmem_limit_bytes=62 * 1024 * 1024
        ),
        name="decode_attention",
    )(
        hidden_in,
        ln_gain.reshape(1, COLS),
        jnp.transpose(w_qkv, (1, 0, 2)),
        k_cache.reshape(HEADS, SPAN, HD),
        v_cache.reshape(HEADS, SPAN, HD),
        w_out.T,
        slopes.reshape(1, HEADS),
        lengths.reshape(1, 1),
    )


def solution(mesh):
    in_specs = (
        P("gy", "gx"),
        P("gx"),
        P("gx", None, "gy"),
        P("gy"),
        P("gx", "gy", None, None),
        P("gx", "gy", None, None),
        P("gx"),
        P("gy", "gx"),
    )
    out_specs = P("gy", "gx")
    return jax.shard_map(local, mesh=mesh, in_specs=in_specs, out_specs=out_specs, check_vma=False)
```

```python
import jax
import jax.numpy as jnp
from jax import lax
from jax.experimental import pallas as pl
from jax.experimental.pallas import tpu as pltpu
from jax.sharding import PartitionSpec as P

D = 14336
GX, GY = 32, 16
ROWS, COLS = 32, 448
HEADS, HD, SPAN = 4, 128, 1024
F32, BF16 = jnp.float32, jnp.bfloat16

CORE, YHI, Z = 16, 32, 64


def far_first(masks):
    def hops(mask):
        ring = (0, 1, 2, 3, 4, 3, 2, 3)
        y = (mask >> 3 & 4) + (mask >> 2 & 3)
        return ring[mask >> 6] + ring[y] + (0, 1, 2, 1)[mask & 3]

    return tuple(sorted(masks, key=hops, reverse=True))


M_ZC = far_first(16 * c + 64 * z for z in range(8) for c in range(2) if c + z)
M_XY = far_first(32 * y + g for y in range(2) for g in range(16) if y + g)
M_GY = far_first(range(1, 16))
M_ZY = far_first(32 * i for i in range(1, 16))
M_GX = far_first(16 * i for i in range(1, 32))


def kernel(
    x_hbm, gain_hbm, w_hbm, k_hbm, v_hbm, wo_hbm, slopes_hbm, lengths_hbm, out_ref,
    x_v, gain_v, w_v, k_v, k_t, v_v, wo_v, wo_t, slopes_v, lengths_v,
    xrecv, a_send, a_recv, b_recv, xs, st,
    part, sib, zy_send, zy_recv, h_recv, h_flat, o_send, o_recv,
    local_sem, send_sem, recv_sem,
):
    gx, gy = lax.axis_index("gx"), lax.axis_index("gy")
    me = gx * GY + gy
    core = gx & 1

    def load(n, src, dst):
        copy = pltpu.make_async_copy(src, dst, local_sem.at[n])
        copy.start()
        return copy

    def send(n, src, dst, mask):
        pltpu.make_async_remote_copy(
            src_ref=src, dst_ref=dst, send_sem=send_sem.at[n], recv_sem=recv_sem.at[n],
            device_id=me ^ mask, device_id_type=pl.DeviceIdType.LOGICAL,
        ).start()

    def arrived(n, ref):
        pltpu.make_async_copy(ref, ref, recv_sem.at[n]).wait()

    def sent(n, ref):
        pltpu.make_async_copy(ref, ref, send_sem.at[n]).wait()

    get_x = load(0, x_hbm, x_v)
    barrier = pltpu.get_barrier_semaphore()
    for mask in far_first(M_ZC + M_XY):
        pl.semaphore_signal(
            barrier, inc=1, device_id=me ^ mask, device_id_type=pl.DeviceIdType.LOGICAL
        )
    get_gain = load(1, gain_hbm, gain_v)
    get_w = [load(2 + c, w_hbm.at[c], w_v.at[c]) for c in range(3)]
    get_k = [load(5 + h, k_hbm.at[h], k_v.at[h]) for h in range(HEADS)]
    get_v = [load(9 + h, v_hbm.at[h], v_v.at[:, pl.ds(h * HD, HD)]) for h in range(HEADS)]
    get_wo = load(13, wo_hbm, wo_v)
    get_slopes = load(14, slopes_hbm, slopes_v)
    get_lengths = load(15, lengths_hbm, lengths_v)

    get_x.wait()
    xf = x_v[...].astype(F32)
    low2 = lax.broadcasted_iota(jnp.int32, (2, 128), 1) < 64
    stats = jnp.where(
        low2, jnp.sum(xf, axis=1, keepdims=True), jnp.sum(xf * xf, axis=1, keepdims=True)
    )
    a_send[0] = stats
    xrecv[gy] = x_v[...]
    pl.semaphore_wait(barrier, len(M_ZC) + len(M_XY))

    for mask in M_GY:
        send(1, x_v, xrecv.at[gy], mask)
    for n, mask in enumerate(M_ZC):
        send(0, a_send.at[0], a_recv.at[n], mask)
    arrived(0, a_recv)
    stats = stats + jnp.sum(a_recv[...], axis=0)

    slot = ((gx >> 1) & 1) * GY + gy
    a_send[1] = stats
    b_recv[slot] = stats
    for mask in M_XY:
        send(2, a_send.at[1], b_recv.at[slot], mask)
    arrived(1, xrecv.at[pl.ds(0, GY - 1)])
    for j in range(GY):
        rows = xrecv[j].astype(F32)
        for t in range(2):
            xs[t * GY + j : t * GY + j + 1, :] = rows[t : t + 1]
    get_gain.wait()
    for c in get_w:
        c.wait()
    arrived(2, b_recv.at[pl.ds(0, 2 * GY - 1)])
    for j in range(GY):
        both = b_recv[j] + b_recv[GY + j]
        for t in range(2):
            st[t * GY + j : t * GY + j + 1, :] = both[t : t + 1, :]
    tot = st[...]
    other = pltpu.roll(tot, 64, 1)
    low = lax.broadcasted_iota(jnp.int32, (ROWS, 128), 1) < 64
    mean = jnp.where(low, tot, other) * (1.0 / D)
    var = jnp.where(low, other, tot) * (1.0 / D) - mean * mean
    rstd = lax.rsqrt(var + 1e-05)
    pieces = []
    for c in range(0, COLS, 128):
        wide = min(128, COLS - c)
        piece = (xs[:, c : c + wide] - mean[:, :wide]) * rstd[:, :wide]
        pieces.append((piece * gain_v[:, c : c + wide]).astype(BF16))
    normed = jnp.concatenate(pieces, axis=1)

    for c in range(3):
        res = jnp.dot(normed, w_v[c], preferred_element_type=F32)
        part[c, 0] = res[:GY]
        part[c, 1] = res[GY:]
        send(3 + c, part.at[c, 1 - core], sib.at[c], CORE)
    for c in range(3):
        arrived(3 + c, sib.at[c])
        mine = part[c, core] + sib[c]
        for h in range(HEADS):
            zy_send[:, c * HEADS + h, :] = mine[:, h * HD : (h + 1) * HD]
    own_slot = gx >> 1
    for n, mask in enumerate(M_ZY):
        send(6, zy_send.at[own_slot ^ (mask >> 5)], zy_recv.at[n], mask)

    get_slopes.wait()
    get_lengths.wait()
    length = lengths_v[...]
    diagonal = lax.broadcasted_iota(jnp.int32, (8, HEADS), 0) == lax.broadcasted_iota(
        jnp.int32, (8, HEADS), 1
    )
    slope = jnp.sum(jnp.where(diagonal, slopes_v[...], 0.0), axis=1, keepdims=True)
    position = lax.broadcasted_iota(jnp.int32, (8, SPAN), 1)
    valid = position < length
    bias = slope * (length - position).astype(F32)
    for h in range(HEADS):
        get_k[h].wait()
        k_t[h * HD : (h + 1) * HD, :] = k_v[h].T
    get_wo.wait()
    wo_t[...] = wo_v[...].T
    for c in get_v:
        c.wait()
    arrived(6, zy_recv)
    qkv = (zy_send[own_slot] + jnp.sum(zy_recv[...], axis=0)).astype(BF16).astype(F32)
    q, k_new, v_new = qkv[0:4], qkv[4:8], qkv[8:12]
    scale = 1.0 / jnp.sqrt(jnp.float32(HD))
    row4 = lax.broadcasted_iota(jnp.int32, (HEADS, HD), 0)
    q_blocks = jnp.concatenate([jnp.where(row4 == h, q, 0.0) for h in range(HEADS)], axis=1)
    q_blocks = jnp.concatenate([q_blocks, jnp.zeros_like(q_blocks)], axis=0).astype(BF16)
    scores = jnp.dot(q_blocks, k_t[...], preferred_element_type=F32) * scale - bias
    scores = jnp.where(valid, scores, -1e30)
    own = jnp.sum(q * k_new, axis=1, keepdims=True) * scale
    own = jnp.concatenate([own, jnp.zeros_like(own)], axis=0)
    top = jnp.maximum(jnp.max(scores, axis=1, keepdims=True), own)
    weights = jnp.where(valid, jnp.exp(scores - top), 0.0).astype(BF16)
    own_weight = jnp.exp(own - top).astype(BF16).astype(F32)
    total = jnp.sum(weights.astype(F32), axis=1, keepdims=True) + own_weight
    mixed = jnp.dot(weights, v_v[...], preferred_element_type=F32)
    acc = own_weight[:HEADS] * v_new
    for h in range(HEADS):
        acc = acc + jnp.where(row4 == h, mixed[:HEADS, h * HD : (h + 1) * HD], 0.0)
    heads = (acc / total[:HEADS]).astype(BF16)

    h_recv[gx] = heads
    for mask in M_GX:
        send(7, h_recv.at[gx], h_recv.at[gx], mask)
    arrived(7, h_recv.at[pl.ds(0, GX - 1)])
    for r in range(GX):
        h_flat[r * HEADS : (r + 1) * HEADS, :] = h_recv[r].astype(F32)
    lhs = jnp.concatenate(
        [h_flat[pl.ds(h, GX, stride=HEADS), :].astype(BF16) for h in range(HEADS)], axis=1
    )
    res = jnp.dot(lhs, wo_t[...], preferred_element_type=F32)

    for j in range(GY):
        o_send[j] = res[2 * j : 2 * j + 2]
    for n, mask in enumerate(M_GY):
        send(8, o_send.at[gy ^ mask], o_recv.at[n], mask)
    arrived(8, o_recv)
    out_ref[...] = (o_send[gy] + jnp.sum(o_recv[...], axis=0)).astype(BF16)

    sent(0, a_recv)
    sent(1, xrecv.at[pl.ds(0, GY - 1)])
    sent(2, b_recv.at[pl.ds(0, 2 * GY - 1)])
    for c in range(3):
        sent(3 + c, sib.at[c])
    sent(6, zy_recv)
    sent(7, h_recv.at[pl.ds(0, GX - 1)])
    sent(8, o_recv)


def local(hidden_in, ln_gain, w_qkv, slopes, k_cache, v_cache, lengths, w_out):
    hbm = pl.BlockSpec(memory_space=pltpu.HBM)
    return pl.pallas_call(
        kernel,
        out_shape=pltpu.VMEM((2, COLS), BF16),
        in_specs=[hbm] * 8,
        out_specs=pl.BlockSpec(memory_space=pltpu.VMEM),
        scratch_shapes=[
            pltpu.VMEM((2, COLS), BF16),
            pltpu.VMEM((1, COLS), F32),
            pltpu.VMEM((3, COLS, HEADS * HD), BF16),
            pltpu.VMEM((HEADS, SPAN, HD), BF16),
            pltpu.VMEM((HEADS * HD, SPAN), BF16),
            pltpu.VMEM((SPAN, HEADS * HD), BF16),
            pltpu.VMEM((COLS, HEADS * HD), BF16),
            pltpu.VMEM((HEADS * HD, COLS), BF16),
            pltpu.VMEM((1, HEADS), F32),
            pltpu.VMEM((1, 1), jnp.int32),
            pltpu.VMEM((GY, 2, COLS), BF16),
            pltpu.VMEM((2, 2, 128), F32),
            pltpu.VMEM((len(M_ZC), 2, 128), F32),
            pltpu.VMEM((2 * GY, 2, 128), F32),
            pltpu.VMEM((ROWS, COLS), F32),
            pltpu.VMEM((ROWS, 128), F32),
            pltpu.VMEM((3, 2, GY, HEADS * HD), F32),
            pltpu.VMEM((3, GY, HEADS * HD), F32),
            pltpu.VMEM((GY, 3 * HEADS, HD), F32),
            pltpu.VMEM((len(M_ZY), 3 * HEADS, HD), F32),
            pltpu.VMEM((GX, HEADS, HD), BF16),
            pltpu.VMEM((GX * HEADS, HD), F32),
            pltpu.VMEM((GY, 2, COLS), F32),
            pltpu.VMEM((len(M_GY), 2, COLS), F32),
            pltpu.SemaphoreType.DMA((16,)),
            pltpu.SemaphoreType.DMA((9,)),
            pltpu.SemaphoreType.DMA((9,)),
        ],
        compiler_params=pltpu.CompilerParams(
            collective_id=0, has_side_effects=True, vmem_limit_bytes=62 * 1024 * 1024
        ),
        name="decode_attention",
    )(
        hidden_in,
        ln_gain.reshape(1, COLS),
        jnp.transpose(w_qkv, (1, 0, 2)),
        k_cache.reshape(HEADS, SPAN, HD),
        v_cache.reshape(HEADS, SPAN, HD),
        w_out.T,
        slopes.reshape(1, HEADS),
        lengths.reshape(1, 1),
    )


def solution(mesh):
    in_specs = (
        P("gy", "gx"),
        P("gx"),
        P("gx", None, "gy"),
        P("gy"),
        P("gx", "gy", None, None),
        P("gx", "gy", None, None),
        P("gx"),
        P("gy", "gx"),
    )
    out_specs = P("gy", "gx")
    return jax.shard_map(local, mesh=mesh, in_specs=in_specs, out_specs=out_specs, check_vma=False)
```

```python
import jax
import jax.numpy as jnp
from jax import lax
from jax.experimental import pallas as pl
from jax.experimental.pallas import tpu as pltpu
from jax.sharding import PartitionSpec as P

D = 14336
GX, GY = 32, 16
ROWS, COLS = 32, 448
HEADS, HD, SPAN = 4, 128, 1024
HALF = HEADS * HD // 2
F32, BF16 = jnp.float32, jnp.bfloat16

CORE, YHI, Z = 16, 32, 64


def far_first(masks):
    def hops(mask):
        ring = (0, 1, 2, 3, 4, 3, 2, 3)
        y = (mask >> 3 & 4) + (mask >> 2 & 3)
        return ring[mask >> 6] + ring[y] + (0, 1, 2, 1)[mask & 3]

    return tuple(sorted(masks, key=hops, reverse=True))


M_ZC = far_first(16 * c + 64 * z for z in range(8) for c in range(2) if c + z)
M_XY = far_first(32 * y + g for y in range(2) for g in range(16) if y + g)
M_GY = far_first(range(1, 16))
M_GX = far_first(16 * i for i in range(1, 32))


def kernel(
    x_hbm, gain_hbm, w_hbm, k_hbm, v_hbm, wo_hbm, slopes_hbm, lengths_hbm, out_ref,
    x_v, gain_v, w_v, k_v, k_t, v_v, wo_v, wo_t, slopes_v, lengths_v,
    xrecv, a_send, a_recv, b_recv, xs, st,
    g_send, g_recv, h_recv, h_flat, o_send, o_recv,
    local_sem, send_sem, recv_sem,
):
    gx, gy = lax.axis_index("gx"), lax.axis_index("gy")
    me = gx * GY + gy
    core = gx & 1

    def load(n, src, dst):
        copy = pltpu.make_async_copy(src, dst, local_sem.at[n])
        copy.start()
        return copy

    def send(n, src, dst, mask):
        pltpu.make_async_remote_copy(
            src_ref=src, dst_ref=dst, send_sem=send_sem.at[n], recv_sem=recv_sem.at[n],
            device_id=me ^ mask, device_id_type=pl.DeviceIdType.LOGICAL,
        ).start()

    def arrived(n, ref):
        pltpu.make_async_copy(ref, ref, recv_sem.at[n]).wait()

    def sent(n, ref):
        pltpu.make_async_copy(ref, ref, send_sem.at[n]).wait()

    get_x = load(0, x_hbm, x_v)
    barrier = pltpu.get_barrier_semaphore()
    for mask in far_first(M_ZC + M_XY):
        pl.semaphore_signal(
            barrier, inc=1, device_id=me ^ mask, device_id_type=pl.DeviceIdType.LOGICAL
        )
    get_gain = load(1, gain_hbm, gain_v.at[core])

    def half(n):
        return pl.ds(pl.multiple_of(n * HALF, HALF), HALF)

    get_w = [load(2 + c, w_hbm.at[c, :, half(core)], w_v.at[core, c]) for c in range(3)]
    get_k = [load(5 + h, k_hbm.at[h], k_v.at[h]) for h in range(HEADS)]
    get_v = [load(9 + h, v_hbm.at[h], v_v.at[:, pl.ds(h * HD, HD)]) for h in range(HEADS)]
    get_wo = load(13, wo_hbm, wo_v)
    get_slopes = load(14, slopes_hbm, slopes_v)
    get_lengths = load(15, lengths_hbm, lengths_v)

    get_x.wait()
    xf = x_v[...].astype(F32)
    low2 = lax.broadcasted_iota(jnp.int32, (2, 128), 1) < 64
    stats = jnp.where(
        low2, jnp.sum(xf, axis=1, keepdims=True), jnp.sum(xf * xf, axis=1, keepdims=True)
    )
    a_send[0] = stats
    xrecv[core, gy] = x_v[...]
    pl.semaphore_wait(barrier, len(M_ZC) + len(M_XY))

    for mask in M_GY:
        send(1, x_v, xrecv.at[core, gy], mask)
    for n, mask in enumerate(M_ZC):
        send(0, a_send.at[0], a_recv.at[n], mask)
    for c in range(3):
        send(3 + c, w_hbm.at[c, :, half(1 - core)], w_v.at[core, c], CORE)
    get_gain.wait()
    send(9, gain_v.at[core], gain_v.at[core], CORE)
    arrived(0, a_recv)
    stats = stats + jnp.sum(a_recv[...], axis=0)

    slot = ((gx >> 1) & 1) * GY + gy
    a_send[1] = stats
    b_recv[slot] = stats
    for mask in M_XY:
        send(2, a_send.at[1], b_recv.at[slot], mask)
    arrived(1, xrecv.at[0, pl.ds(0, GY - 1)])
    send(10, xrecv.at[core], xrecv.at[core], CORE)
    for c in get_w:
        c.wait()
    for c in range(3):
        arrived(3 + c, w_v.at[0, c])
    arrived(9, gain_v.at[0])
    arrived(10, xrecv.at[0])
    for k in range(2):
        for j in range(GY):
            xs[k, 2 * j : 2 * j + 2, :] = xrecv[k, j].astype(F32)
    arrived(2, b_recv.at[pl.ds(0, 2 * GY - 1)])
    for j in range(GY):
        st[2 * j : 2 * j + 2, :] = b_recv[j] + b_recv[GY + j]
    tot = st[...]
    other = pltpu.roll(tot, 64, 1)
    low = lax.broadcasted_iota(jnp.int32, (ROWS, 128), 1) < 64
    mean = jnp.where(low, tot, other) * (1.0 / D)
    var = jnp.where(low, other, tot) * (1.0 / D) - mean * mean
    rstd = lax.rsqrt(var + 1e-05)
    normed = []
    for k in range(2):
        pieces = []
        for c in range(0, COLS, 128):
            wide = min(128, COLS - c)
            piece = (xs[k, :, c : c + wide] - mean[:, :wide]) * rstd[:, :wide]
            pieces.append((piece * gain_v[k, :, c : c + wide]).astype(BF16))
        normed.append(jnp.concatenate(pieces, axis=1))

    for c in range(3):
        res = jnp.dot(normed[0], w_v[0, c], preferred_element_type=F32)
        res = res + jnp.dot(normed[1], w_v[1, c], preferred_element_type=F32)
        for h in range(2):
            g_send[:, c * 2 + h, :] = res[:, h * HD : (h + 1) * HD]
    for mask in M_GX:
        n = (mask // CORE % 2) * GY + mask // YHI
        send(6, g_send.at[gx ^ (mask // CORE)], g_recv.at[n], mask)
    g_recv[0] = g_send[gx]

    get_slopes.wait()
    get_lengths.wait()
    length = lengths_v[...]
    diagonal = lax.broadcasted_iota(jnp.int32, (8, HEADS), 0) == lax.broadcasted_iota(
        jnp.int32, (8, HEADS), 1
    )
    slope = jnp.sum(jnp.where(diagonal, slopes_v[...], 0.0), axis=1, keepdims=True)
    position = lax.broadcasted_iota(jnp.int32, (8, SPAN), 1)
    valid = position < length
    bias = slope * (length - position).astype(F32)
    for h in range(HEADS):
        get_k[h].wait()
        k_t[h * HD : (h + 1) * HD, :] = k_v[h].T
    get_wo.wait()
    wo_t[...] = wo_v[...].T
    for c in get_v:
        c.wait()
    arrived(6, g_recv.at[pl.ds(1, GX - 1)])
    same = jnp.sum(g_recv[0:GY], axis=0)
    other = jnp.sum(g_recv[GY:GX], axis=0)
    first = jnp.where(core == 0, same, other)
    second = jnp.where(core == 0, other, same)
    q, k_new, v_new = [
        jnp.concatenate([first[2 * c : 2 * c + 2], second[2 * c : 2 * c + 2]], axis=0)
        .astype(BF16)
        .astype(F32)
        for c in range(3)
    ]
    scale = 1.0 / jnp.sqrt(jnp.float32(HD))
    row4 = lax.broadcasted_iota(jnp.int32, (HEADS, HD), 0)
    q_blocks = jnp.concatenate([jnp.where(row4 == h, q, 0.0) for h in range(HEADS)], axis=1)
    q_blocks = jnp.concatenate([q_blocks, jnp.zeros_like(q_blocks)], axis=0).astype(BF16)
    scores = jnp.dot(q_blocks, k_t[...], preferred_element_type=F32) * scale - bias
    scores = jnp.where(valid, scores, -1e30)
    own = jnp.sum(q * k_new, axis=1, keepdims=True) * scale
    own = jnp.concatenate([own, jnp.zeros_like(own)], axis=0)
    top = jnp.maximum(jnp.max(scores, axis=1, keepdims=True), own)
    weights = jnp.where(valid, jnp.exp(scores - top), 0.0).astype(BF16)
    own_weight = jnp.exp(own - top).astype(BF16).astype(F32)
    total = jnp.sum(weights.astype(F32), axis=1, keepdims=True) + own_weight
    mixed = jnp.dot(weights, v_v[...], preferred_element_type=F32)
    acc = own_weight[:HEADS] * v_new
    for h in range(HEADS):
        acc = acc + jnp.where(row4 == h, mixed[:HEADS, h * HD : (h + 1) * HD], 0.0)
    heads = (acc / total[:HEADS]).astype(BF16)

    h_recv[gx] = heads
    for mask in M_GX:
        send(7, h_recv.at[gx], h_recv.at[gx], mask)
    arrived(7, h_recv.at[pl.ds(0, GX - 1)])
    for r in range(GX):
        h_flat[r * HEADS : (r + 1) * HEADS, :] = h_recv[r].astype(F32)
    lhs = jnp.concatenate(
        [h_flat[pl.ds(h, GX, stride=HEADS), :].astype(BF16) for h in range(HEADS)], axis=1
    )
    res = jnp.dot(lhs, wo_t[...], preferred_element_type=F32)

    for j in range(GY):
        o_send[j] = res[2 * j : 2 * j + 2]
    for n, mask in enumerate(M_GY):
        send(8, o_send.at[gy ^ mask], o_recv.at[n], mask)
    arrived(8, o_recv)
    out_ref[...] = (o_send[gy] + jnp.sum(o_recv[...], axis=0)).astype(BF16)

    sent(0, a_recv)
    sent(1, xrecv.at[0, pl.ds(0, GY - 1)])
    sent(2, b_recv.at[pl.ds(0, 2 * GY - 1)])
    for c in range(3):
        sent(3 + c, w_v.at[0, c])
    sent(6, g_recv.at[pl.ds(1, GX - 1)])
    sent(9, gain_v.at[0])
    sent(10, xrecv.at[0])
    sent(7, h_recv.at[pl.ds(0, GX - 1)])
    sent(8, o_recv)


def local(hidden_in, ln_gain, w_qkv, slopes, k_cache, v_cache, lengths, w_out):
    hbm = pl.BlockSpec(memory_space=pltpu.HBM)
    return pl.pallas_call(
        kernel,
        out_shape=pltpu.VMEM((2, COLS), BF16),
        in_specs=[hbm] * 8,
        out_specs=pl.BlockSpec(memory_space=pltpu.VMEM),
        scratch_shapes=[
            pltpu.VMEM((2, COLS), BF16),
            pltpu.VMEM((2, 1, COLS), F32),
            pltpu.VMEM((2, 3, COLS, HALF), BF16),
            pltpu.VMEM((HEADS, SPAN, HD), BF16),
            pltpu.VMEM((HEADS * HD, SPAN), BF16),
            pltpu.VMEM((SPAN, HEADS * HD), BF16),
            pltpu.VMEM((COLS, HEADS * HD), BF16),
            pltpu.VMEM((HEADS * HD, COLS), BF16),
            pltpu.VMEM((1, HEADS), F32),
            pltpu.VMEM((1, 1), jnp.int32),
            pltpu.VMEM((2, GY, 2, COLS), BF16),
            pltpu.VMEM((2, 2, 128), F32),
            pltpu.VMEM((len(M_ZC), 2, 128), F32),
            pltpu.VMEM((2 * GY, 2, 128), F32),
            pltpu.VMEM((2, ROWS, COLS), F32),
            pltpu.VMEM((ROWS, 128), F32),
            pltpu.VMEM((GX, 3 * HEADS // 2, HD), F32),
            pltpu.VMEM((GX, 3 * HEADS // 2, HD), F32),
            pltpu.VMEM((GX, HEADS, HD), BF16),
            pltpu.VMEM((GX * HEADS, HD), F32),
            pltpu.VMEM((GY, 2, COLS), F32),
            pltpu.VMEM((len(M_GY), 2, COLS), F32),
            pltpu.SemaphoreType.DMA((16,)),
            pltpu.SemaphoreType.DMA((11,)),
            pltpu.SemaphoreType.DMA((11,)),
        ],
        compiler_params=pltpu.CompilerParams(
            collective_id=0, has_side_effects=True, vmem_limit_bytes=62 * 1024 * 1024
        ),
        name="decode_attention",
    )(
        hidden_in,
        ln_gain.reshape(1, COLS),
        jnp.transpose(w_qkv, (1, 0, 2)),
        k_cache.reshape(HEADS, SPAN, HD),
        v_cache.reshape(HEADS, SPAN, HD),
        w_out.T,
        slopes.reshape(1, HEADS),
        lengths.reshape(1, 1),
    )


def solution(mesh):
    in_specs = (
        P("gy", "gx"),
        P("gx"),
        P("gx", None, "gy"),
        P("gy"),
        P("gx", "gy", None, None),
        P("gx", "gy", None, None),
        P("gx"),
        P("gy", "gx"),
    )
    out_specs = P("gy", "gx")
    return jax.shard_map(local, mesh=mesh, in_specs=in_specs, out_specs=out_specs, check_vma=False)
```

```python
import jax
import jax.numpy as jnp
from jax import lax
from jax.experimental import pallas as pl
from jax.experimental.pallas import tpu as pltpu
from jax.sharding import PartitionSpec as P

D = 14336
GX, GY = 32, 16
ROWS, COLS = 32, 448
HEADS, HD, SPAN = 4, 128, 1024
HALF = HEADS * HD // 2
F32, BF16 = jnp.float32, jnp.bfloat16

CORE, YHI, Z = 16, 32, 64


def far_first(masks):
    def hops(mask):
        ring = (0, 1, 2, 3, 4, 3, 2, 3)
        y = (mask >> 3 & 4) + (mask >> 2 & 3)
        return ring[mask >> 6] + ring[y] + (0, 1, 2, 1)[mask & 3]

    return tuple(sorted(masks, key=hops, reverse=True))


M_ZC = far_first(16 * c + 64 * z for z in range(8) for c in range(2) if c + z)
M_XY = far_first(32 * y + g for y in range(2) for g in range(16) if y + g)
M_GY = far_first(range(1, 16))
M_GX = far_first(16 * i for i in range(1, 32))


def kernel(
    x_hbm, gain_hbm, w_hbm, k_hbm, v_hbm, wo_hbm, slopes_hbm, lengths_hbm, out_ref,
    x_v, gain_v, w_v, k_v, k_t, v_v, wo_v, wo_t, slopes_v, lengths_v,
    xrecv, a_send, a_recv, b_recv, xs, st,
    g_send, g_recv, h_recv, h_flat, o_send, o_recv,
    local_sem, send_sem, recv_sem,
):
    gx, gy = lax.axis_index("gx"), lax.axis_index("gy")
    me = gx * GY + gy
    core = gx & 1

    def load(n, src, dst):
        copy = pltpu.make_async_copy(src, dst, local_sem.at[n])
        copy.start()
        return copy

    def send(n, src, dst, mask):
        pltpu.make_async_remote_copy(
            src_ref=src, dst_ref=dst, send_sem=send_sem.at[n], recv_sem=recv_sem.at[n],
            device_id=me ^ mask, device_id_type=pl.DeviceIdType.LOGICAL,
        ).start()

    def arrived(n, ref):
        pltpu.make_async_copy(ref, ref, recv_sem.at[n]).wait()

    def sent(n, ref):
        pltpu.make_async_copy(ref, ref, send_sem.at[n]).wait()

    get_x = load(0, x_hbm, x_v)
    barrier = pltpu.get_barrier_semaphore()
    for mask in far_first(M_ZC + M_XY):
        pl.semaphore_signal(
            barrier, inc=1, device_id=me ^ mask, device_id_type=pl.DeviceIdType.LOGICAL
        )
    get_gain = load(1, gain_hbm, gain_v.at[core])

    def half(n):
        return pl.ds(pl.multiple_of(n * HALF, HALF), HALF)

    get_w = [load(2 + c, w_hbm.at[c, :, half(core)], w_v.at[core, c]) for c in range(3)]
    get_k = [load(5 + h, k_hbm.at[h], k_v.at[h]) for h in range(HEADS)]
    get_v = [load(9 + h, v_hbm.at[h], v_v.at[:, pl.ds(h * HD, HD)]) for h in range(HEADS)]
    get_wo = load(13, wo_hbm, wo_v)
    get_slopes = load(14, slopes_hbm, slopes_v)
    get_lengths = load(15, lengths_hbm, lengths_v)

    get_x.wait()
    xf = x_v[...].astype(F32)
    low2 = lax.broadcasted_iota(jnp.int32, (2, 128), 1) < 64
    stats = jnp.where(
        low2, jnp.sum(xf, axis=1, keepdims=True), jnp.sum(xf * xf, axis=1, keepdims=True)
    )
    a_send[0] = stats
    xrecv[core, gy] = x_v[...]
    pl.semaphore_wait(barrier, len(M_ZC) + len(M_XY))

    for mask in M_GY:
        send(1, x_v, xrecv.at[core, gy], mask)
    for n, mask in enumerate(M_ZC):
        send(0, a_send.at[0], a_recv.at[n], mask)
    arrived(0, a_recv)
    stats = stats + jnp.sum(a_recv[...], axis=0)

    slot = ((gx >> 1) & 1) * GY + gy
    a_send[1] = stats
    b_recv[slot] = stats
    for mask in M_XY:
        send(2, a_send.at[1], b_recv.at[slot], mask)
    for c in range(3):
        send(3 + c, w_hbm.at[c, :, half(1 - core)], w_v.at[core, c], CORE)
    get_gain.wait()
    send(9, gain_v.at[core], gain_v.at[core], CORE)
    arrived(1, xrecv.at[0, pl.ds(0, GY - 1)])
    send(10, xrecv.at[core], xrecv.at[core], CORE)
    for c in get_w:
        c.wait()
    for c in range(3):
        arrived(3 + c, w_v.at[0, c])
    arrived(9, gain_v.at[0])
    arrived(10, xrecv.at[0])
    for k in range(2):
        for j in range(GY):
            xs[k, 2 * j : 2 * j + 2, :] = xrecv[k, j].astype(F32)
    arrived(2, b_recv.at[pl.ds(0, 2 * GY - 1)])
    for j in range(GY):
        st[2 * j : 2 * j + 2, :] = b_recv[j] + b_recv[GY + j]
    tot = st[...]
    other = pltpu.roll(tot, 64, 1)
    low = lax.broadcasted_iota(jnp.int32, (ROWS, 128), 1) < 64
    mean = jnp.where(low, tot, other) * (1.0 / D)
    var = jnp.where(low, other, tot) * (1.0 / D) - mean * mean
    rstd = lax.rsqrt(var + 1e-05)
    normed = []
    for k in range(2):
        pieces = []
        for c in range(0, COLS, 128):
            wide = min(128, COLS - c)
            piece = (xs[k, :, c : c + wide] - mean[:, :wide]) * rstd[:, :wide]
            pieces.append((piece * gain_v[k, :, c : c + wide]).astype(BF16))
        normed.append(jnp.concatenate(pieces, axis=1))

    for c in range(3):
        res = jnp.dot(normed[0], w_v[0, c], preferred_element_type=F32)
        res = res + jnp.dot(normed[1], w_v[1, c], preferred_element_type=F32)
        for h in range(2):
            g_send[:, c * 2 + h, :] = res[:, h * HD : (h + 1) * HD]
    for mask in M_GX:
        n = (mask // CORE % 2) * GY + mask // YHI
        send(6, g_send.at[gx ^ (mask // CORE)], g_recv.at[n], mask)
    g_recv[0] = g_send[gx]

    get_slopes.wait()
    get_lengths.wait()
    length = lengths_v[...]
    diagonal = lax.broadcasted_iota(jnp.int32, (8, HEADS), 0) == lax.broadcasted_iota(
        jnp.int32, (8, HEADS), 1
    )
    slope = jnp.sum(jnp.where(diagonal, slopes_v[...], 0.0), axis=1, keepdims=True)
    position = lax.broadcasted_iota(jnp.int32, (8, SPAN), 1)
    valid = position < length
    bias = slope * (length - position).astype(F32)
    for h in range(HEADS):
        get_k[h].wait()
        k_t[h * HD : (h + 1) * HD, :] = k_v[h].T
    get_wo.wait()
    wo_t[...] = wo_v[...].T
    for c in get_v:
        c.wait()
    arrived(6, g_recv.at[pl.ds(1, GX - 1)])
    same = jnp.sum(g_recv[0:GY], axis=0)
    other = jnp.sum(g_recv[GY:GX], axis=0)
    first = jnp.where(core == 0, same, other)
    second = jnp.where(core == 0, other, same)
    q, k_new, v_new = [
        jnp.concatenate([first[2 * c : 2 * c + 2], second[2 * c : 2 * c + 2]], axis=0)
        .astype(BF16)
        .astype(F32)
        for c in range(3)
    ]
    scale = 1.0 / jnp.sqrt(jnp.float32(HD))
    row4 = lax.broadcasted_iota(jnp.int32, (HEADS, HD), 0)
    q_blocks = jnp.concatenate([jnp.where(row4 == h, q, 0.0) for h in range(HEADS)], axis=1)
    q_blocks = jnp.concatenate([q_blocks, jnp.zeros_like(q_blocks)], axis=0).astype(BF16)
    scores = jnp.dot(q_blocks, k_t[...], preferred_element_type=F32) * scale - bias
    scores = jnp.where(valid, scores, -1e30)
    own = jnp.sum(q * k_new, axis=1, keepdims=True) * scale
    own = jnp.concatenate([own, jnp.zeros_like(own)], axis=0)
    top = jnp.maximum(jnp.max(scores, axis=1, keepdims=True), own)
    weights = jnp.where(valid, jnp.exp(scores - top), 0.0).astype(BF16)
    own_weight = jnp.exp(own - top).astype(BF16).astype(F32)
    total = jnp.sum(weights.astype(F32), axis=1, keepdims=True) + own_weight
    mixed = jnp.dot(weights, v_v[...], preferred_element_type=F32)
    acc = own_weight[:HEADS] * v_new
    for h in range(HEADS):
        acc = acc + jnp.where(row4 == h, mixed[:HEADS, h * HD : (h + 1) * HD], 0.0)
    heads = (acc / total[:HEADS]).astype(BF16)

    h_recv[gx] = heads
    for mask in M_GX:
        send(7, h_recv.at[gx], h_recv.at[gx], mask)
    arrived(7, h_recv.at[pl.ds(0, GX - 1)])
    for r in range(GX):
        h_flat[r * HEADS : (r + 1) * HEADS, :] = h_recv[r].astype(F32)
    lhs = jnp.concatenate(
        [h_flat[pl.ds(h, GX, stride=HEADS), :].astype(BF16) for h in range(HEADS)], axis=1
    )
    res = jnp.dot(lhs, wo_t[...], preferred_element_type=F32)

    for j in range(GY):
        o_send[j] = res[2 * j : 2 * j + 2]
    for n, mask in enumerate(M_GY):
        send(8, o_send.at[gy ^ mask], o_recv.at[n], mask)
    arrived(8, o_recv)
    out_ref[...] = (o_send[gy] + jnp.sum(o_recv[...], axis=0)).astype(BF16)

    sent(0, a_recv)
    sent(1, xrecv.at[0, pl.ds(0, GY - 1)])
    sent(2, b_recv.at[pl.ds(0, 2 * GY - 1)])
    for c in range(3):
        sent(3 + c, w_v.at[0, c])
    sent(6, g_recv.at[pl.ds(1, GX - 1)])
    sent(9, gain_v.at[0])
    sent(10, xrecv.at[0])
    sent(7, h_recv.at[pl.ds(0, GX - 1)])
    sent(8, o_recv)


def local(hidden_in, ln_gain, w_qkv, slopes, k_cache, v_cache, lengths, w_out):
    hbm = pl.BlockSpec(memory_space=pltpu.HBM)
    return pl.pallas_call(
        kernel,
        out_shape=pltpu.VMEM((2, COLS), BF16),
        in_specs=[hbm] * 8,
        out_specs=pl.BlockSpec(memory_space=pltpu.VMEM),
        scratch_shapes=[
            pltpu.VMEM((2, COLS), BF16),
            pltpu.VMEM((2, 1, COLS), F32),
            pltpu.VMEM((2, 3, COLS, HALF), BF16),
            pltpu.VMEM((HEADS, SPAN, HD), BF16),
            pltpu.VMEM((HEADS * HD, SPAN), BF16),
            pltpu.VMEM((SPAN, HEADS * HD), BF16),
            pltpu.VMEM((COLS, HEADS * HD), BF16),
            pltpu.VMEM((HEADS * HD, COLS), BF16),
            pltpu.VMEM((1, HEADS), F32),
            pltpu.VMEM((1, 1), jnp.int32),
            pltpu.VMEM((2, GY, 2, COLS), BF16),
            pltpu.VMEM((2, 2, 128), F32),
            pltpu.VMEM((len(M_ZC), 2, 128), F32),
            pltpu.VMEM((2 * GY, 2, 128), F32),
            pltpu.VMEM((2, ROWS, COLS), F32),
            pltpu.VMEM((ROWS, 128), F32),
            pltpu.VMEM((GX, 3 * HEADS // 2, HD), F32),
            pltpu.VMEM((GX, 3 * HEADS // 2, HD), F32),
            pltpu.VMEM((GX, HEADS, HD), BF16),
            pltpu.VMEM((GX * HEADS, HD), F32),
            pltpu.VMEM((GY, 2, COLS), F32),
            pltpu.VMEM((len(M_GY), 2, COLS), F32),
            pltpu.SemaphoreType.DMA((16,)),
            pltpu.SemaphoreType.DMA((11,)),
            pltpu.SemaphoreType.DMA((11,)),
        ],
        compiler_params=pltpu.CompilerParams(
            collective_id=0, has_side_effects=True, vmem_limit_bytes=62 * 1024 * 1024
        ),
        name="decode_attention",
    )(
        hidden_in,
        ln_gain.reshape(1, COLS),
        jnp.transpose(w_qkv, (1, 0, 2)),
        k_cache.reshape(HEADS, SPAN, HD),
        v_cache.reshape(HEADS, SPAN, HD),
        w_out.T,
        slopes.reshape(1, HEADS),
        lengths.reshape(1, 1),
    )


def solution(mesh):
    in_specs = (
        P("gy", "gx"),
        P("gx"),
        P("gx", None, "gy"),
        P("gy"),
        P("gx", "gy", None, None),
        P("gx", "gy", None, None),
        P("gx"),
        P("gy", "gx"),
    )
    out_specs = P("gy", "gx")
    return jax.shard_map(local, mesh=mesh, in_specs=in_specs, out_specs=out_specs, check_vma=False)
```

```python
import jax
import jax.numpy as jnp
from jax import lax
from jax.experimental import pallas as pl
from jax.experimental.pallas import tpu as pltpu
from jax.sharding import PartitionSpec as P

D = 14336
GX, GY = 32, 16
ROWS, COLS = 32, 448
HEADS, HD, SPAN = 4, 128, 1024
HALF = HEADS * HD // 2
F32, BF16 = jnp.float32, jnp.bfloat16

CORE, YHI, Z = 16, 32, 64


def far_first(masks):
    def hops(mask):
        ring = (0, 1, 2, 3, 4, 3, 2, 3)
        y = (mask >> 3 & 4) + (mask >> 2 & 3)
        return ring[mask >> 6] + ring[y] + (0, 1, 2, 1)[mask & 3]

    return tuple(sorted(masks, key=hops, reverse=True))


M_ZC = far_first(16 * c + 64 * z for z in range(8) for c in range(2) if c + z)
M_XY = far_first(32 * y + g for y in range(2) for g in range(16) if y + g)
M_GY = far_first(range(1, 16))
M_GX = far_first(16 * i for i in range(1, 32))


def kernel(
    x_hbm, gain_hbm, w_hbm, k_hbm, v_hbm, wo_hbm, slopes_hbm, lengths_hbm, out_ref,
    x_v, gain_v, w_v, k_v, k_t, v_v, wo_v, wo_t, slopes_v, lengths_v,
    xrecv, a_send, a_recv, b_recv, xs, st,
    g_send, g_recv, h_recv, h_flat, o_send, o_recv,
    local_sem, send_sem, recv_sem,
):
    gx, gy = lax.axis_index("gx"), lax.axis_index("gy")
    me = gx * GY + gy
    core = gx & 1

    def load(n, src, dst):
        copy = pltpu.make_async_copy(src, dst, local_sem.at[n])
        copy.start()
        return copy

    def send(n, src, dst, mask):
        pltpu.make_async_remote_copy(
            src_ref=src, dst_ref=dst, send_sem=send_sem.at[n], recv_sem=recv_sem.at[n],
            device_id=me ^ mask, device_id_type=pl.DeviceIdType.LOGICAL,
        ).start()

    def arrived(n, ref):
        pltpu.make_async_copy(ref, ref, recv_sem.at[n]).wait()

    def sent(n, ref):
        pltpu.make_async_copy(ref, ref, send_sem.at[n]).wait()

    get_x = load(0, x_hbm, x_v)
    barrier = pltpu.get_barrier_semaphore()
    for mask in far_first(M_ZC + M_XY):
        pl.semaphore_signal(
            barrier, inc=1, device_id=me ^ mask, device_id_type=pl.DeviceIdType.LOGICAL
        )
    get_gain = load(1, gain_hbm, gain_v.at[core])

    def half(n):
        return pl.ds(pl.multiple_of(n * HALF, HALF), HALF)

    get_w = [load(2 + c, w_hbm.at[c, :, half(core)], w_v.at[core, c]) for c in range(3)]
    get_k = [load(5 + h, k_hbm.at[h], k_v.at[h]) for h in range(HEADS)]
    get_v = [load(9 + h, v_hbm.at[h], v_v.at[:, pl.ds(h * HD, HD)]) for h in range(HEADS)]
    get_wo = load(13, wo_hbm, wo_v)
    get_slopes = load(14, slopes_hbm, slopes_v)
    get_lengths = load(15, lengths_hbm, lengths_v)

    get_x.wait()
    xf = x_v[...].astype(F32)
    low2 = lax.broadcasted_iota(jnp.int32, (2, 128), 1) < 64
    stats = jnp.where(
        low2, jnp.sum(xf, axis=1, keepdims=True), jnp.sum(xf * xf, axis=1, keepdims=True)
    )
    a_send[0] = stats
    xrecv[core, gy] = x_v[...]
    pl.semaphore_wait(barrier, len(M_ZC) + len(M_XY))

    for mask in M_GY:
        send(1, x_v, xrecv.at[core, gy], mask)
    for n, mask in enumerate(M_ZC):
        send(0, a_send.at[0], a_recv.at[n], mask)
    arrived(0, a_recv)
    stats = stats + jnp.sum(a_recv[...], axis=0)

    slot = ((gx >> 1) & 1) * GY + gy
    a_send[1] = stats
    b_recv[slot] = stats
    for mask in M_XY:
        send(2, a_send.at[1], b_recv.at[slot], mask)
    for c in range(3):
        send(3 + c, w_hbm.at[c, :, half(1 - core)], w_v.at[core, c], CORE)
    get_gain.wait()
    send(9, gain_v.at[core], gain_v.at[core], CORE)
    arrived(1, xrecv.at[0, pl.ds(0, GY - 1)])
    send(10, xrecv.at[core], xrecv.at[core], CORE)
    for c in get_w:
        c.wait()
    for c in range(3):
        arrived(3 + c, w_v.at[0, c])
    arrived(9, gain_v.at[0])
    arrived(10, xrecv.at[0])
    for k in range(2):
        for j in range(GY):
            xs[k, 2 * j : 2 * j + 2, :] = xrecv[k, j].astype(F32)
    arrived(2, b_recv.at[pl.ds(0, 2 * GY - 1)])
    for j in range(GY):
        st[2 * j : 2 * j + 2, :] = b_recv[j] + b_recv[GY + j]
    tot = st[...]
    other = pltpu.roll(tot, 64, 1)
    low = lax.broadcasted_iota(jnp.int32, (ROWS, 128), 1) < 64
    mean = jnp.where(low, tot, other) * (1.0 / D)
    var = jnp.where(low, other, tot) * (1.0 / D) - mean * mean
    rstd = lax.rsqrt(var + 1e-05)
    normed = []
    for k in range(2):
        pieces = []
        for c in range(0, COLS, 128):
            wide = min(128, COLS - c)
            piece = (xs[k, :, c : c + wide] - mean[:, :wide]) * rstd[:, :wide]
            pieces.append((piece * gain_v[k, :, c : c + wide]).astype(BF16))
        normed.append(jnp.concatenate(pieces, axis=1))

    for c in range(3):
        res = jnp.dot(normed[0], w_v[0, c], preferred_element_type=F32)
        res = res + jnp.dot(normed[1], w_v[1, c], preferred_element_type=F32)
        for h in range(2):
            g_send[:, c * 2 + h, :] = res[:, h * HD : (h + 1) * HD]
    for mask in M_GX:
        n = (mask // CORE % 2) * GY + mask // YHI
        send(6, g_send.at[gx ^ (mask // CORE)], g_recv.at[n], mask)
    g_recv[0] = g_send[gx]

    get_slopes.wait()
    get_lengths.wait()
    length = lengths_v[...]
    diagonal = lax.broadcasted_iota(jnp.int32, (8, HEADS), 0) == lax.broadcasted_iota(
        jnp.int32, (8, HEADS), 1
    )
    slope = jnp.sum(jnp.where(diagonal, slopes_v[...], 0.0), axis=1, keepdims=True)
    position = lax.broadcasted_iota(jnp.int32, (8, SPAN), 1)
    valid = position < length
    bias = slope * (length - position).astype(F32)
    for h in range(HEADS):
        get_k[h].wait()
        k_t[h * HD : (h + 1) * HD, :] = k_v[h].T
    get_wo.wait()
    wo_t[...] = wo_v[...].T
    for c in get_v:
        c.wait()
    arrived(6, g_recv.at[pl.ds(1, GX - 1)])
    same = jnp.sum(g_recv[0:GY], axis=0)
    other = jnp.sum(g_recv[GY:GX], axis=0)
    first = jnp.where(core == 0, same, other)
    second = jnp.where(core == 0, other, same)
    q, k_new, v_new = [
        jnp.concatenate([first[2 * c : 2 * c + 2], second[2 * c : 2 * c + 2]], axis=0)
        .astype(BF16)
        .astype(F32)
        for c in range(3)
    ]
    scale = 1.0 / jnp.sqrt(jnp.float32(HD))
    row4 = lax.broadcasted_iota(jnp.int32, (HEADS, HD), 0)
    q_blocks = jnp.concatenate([jnp.where(row4 == h, q, 0.0) for h in range(HEADS)], axis=1)
    q_blocks = jnp.concatenate([q_blocks, jnp.zeros_like(q_blocks)], axis=0).astype(BF16)
    scores = jnp.dot(q_blocks, k_t[...], preferred_element_type=F32) * scale - bias
    scores = jnp.where(valid, scores, -1e30)
    own = jnp.sum(q * k_new, axis=1, keepdims=True) * scale
    own = jnp.concatenate([own, jnp.zeros_like(own)], axis=0)
    top = jnp.maximum(jnp.max(scores, axis=1, keepdims=True), own)
    weights = jnp.where(valid, jnp.exp(scores - top), 0.0).astype(BF16)
    own_weight = jnp.exp(own - top).astype(BF16).astype(F32)
    total = jnp.sum(weights.astype(F32), axis=1, keepdims=True) + own_weight
    mixed = jnp.dot(weights, v_v[...], preferred_element_type=F32)
    acc = own_weight[:HEADS] * v_new
    for h in range(HEADS):
        acc = acc + jnp.where(row4 == h, mixed[:HEADS, h * HD : (h + 1) * HD], 0.0)
    heads = (acc / total[:HEADS]).astype(BF16)

    h_recv[gx] = heads
    for mask in M_GX:
        send(7, h_recv.at[gx], h_recv.at[gx], mask)
    arrived(7, h_recv.at[pl.ds(0, GX - 1)])
    for r in range(GX):
        h_flat[r * HEADS : (r + 1) * HEADS, :] = h_recv[r].astype(F32)
    lhs = jnp.concatenate(
        [h_flat[pl.ds(h, GX, stride=HEADS), :].astype(BF16) for h in range(HEADS)], axis=1
    )
    res = jnp.dot(lhs, wo_t[...], preferred_element_type=F32)

    for j in range(GY):
        o_send[j] = res[2 * j : 2 * j + 2]
    for n, mask in enumerate(M_GY):
        send(8, o_send.at[gy ^ mask], o_recv.at[n], mask)
    sent(0, a_recv)
    sent(1, xrecv.at[0, pl.ds(0, GY - 1)])
    sent(2, b_recv.at[pl.ds(0, 2 * GY - 1)])
    for c in range(3):
        sent(3 + c, w_v.at[0, c])
    sent(6, g_recv.at[pl.ds(1, GX - 1)])
    sent(9, gain_v.at[0])
    sent(10, xrecv.at[0])
    sent(7, h_recv.at[pl.ds(0, GX - 1)])
    arrived(8, o_recv)
    out_ref[...] = (o_send[gy] + jnp.sum(o_recv[...], axis=0)).astype(BF16)
    sent(8, o_recv)


def local(hidden_in, ln_gain, w_qkv, slopes, k_cache, v_cache, lengths, w_out):
    hbm = pl.BlockSpec(memory_space=pltpu.HBM)
    return pl.pallas_call(
        kernel,
        out_shape=pltpu.VMEM((2, COLS), BF16),
        in_specs=[hbm] * 8,
        out_specs=pl.BlockSpec(memory_space=pltpu.VMEM),
        scratch_shapes=[
            pltpu.VMEM((2, COLS), BF16),
            pltpu.VMEM((2, 1, COLS), F32),
            pltpu.VMEM((2, 3, COLS, HALF), BF16),
            pltpu.VMEM((HEADS, SPAN, HD), BF16),
            pltpu.VMEM((HEADS * HD, SPAN), BF16),
            pltpu.VMEM((SPAN, HEADS * HD), BF16),
            pltpu.VMEM((COLS, HEADS * HD), BF16),
            pltpu.VMEM((HEADS * HD, COLS), BF16),
            pltpu.VMEM((1, HEADS), F32),
            pltpu.VMEM((1, 1), jnp.int32),
            pltpu.VMEM((2, GY, 2, COLS), BF16),
            pltpu.VMEM((2, 2, 128), F32),
            pltpu.VMEM((len(M_ZC), 2, 128), F32),
            pltpu.VMEM((2 * GY, 2, 128), F32),
            pltpu.VMEM((2, ROWS, COLS), F32),
            pltpu.VMEM((ROWS, 128), F32),
            pltpu.VMEM((GX, 3 * HEADS // 2, HD), F32),
            pltpu.VMEM((GX, 3 * HEADS // 2, HD), F32),
            pltpu.VMEM((GX, HEADS, HD), BF16),
            pltpu.VMEM((GX * HEADS, HD), F32),
            pltpu.VMEM((GY, 2, COLS), F32),
            pltpu.VMEM((len(M_GY), 2, COLS), F32),
            pltpu.SemaphoreType.DMA((16,)),
            pltpu.SemaphoreType.DMA((11,)),
            pltpu.SemaphoreType.DMA((11,)),
        ],
        compiler_params=pltpu.CompilerParams(
            collective_id=0, has_side_effects=True, vmem_limit_bytes=62 * 1024 * 1024
        ),
        name="decode_attention",
    )(
        hidden_in,
        ln_gain.reshape(1, COLS),
        jnp.transpose(w_qkv, (1, 0, 2)),
        k_cache.reshape(HEADS, SPAN, HD),
        v_cache.reshape(HEADS, SPAN, HD),
        w_out.T,
        slopes.reshape(1, HEADS),
        lengths.reshape(1, 1),
    )


def solution(mesh):
    in_specs = (
        P("gy", "gx"),
        P("gx"),
        P("gx", None, "gy"),
        P("gy"),
        P("gx", "gy", None, None),
        P("gx", "gy", None, None),
        P("gx"),
        P("gy", "gx"),
    )
    out_specs = P("gy", "gx")
    return jax.shard_map(local, mesh=mesh, in_specs=in_specs, out_specs=out_specs, check_vma=False)
```
